1024 devices in a mesh: dp: 8 (over y_hi, x), ctx: 128 (over y_lo, z, core).
Axes of the slice: x: 4, y: 4 (y_hi: 2, y_lo: 2; y = y_hi * 2 + y_lo), z: 32, core: 2. Of those that a mesh axis runs over, the one named last changes fastest.
Arguments:
- queries: bfloat16 [131072, 2048], P(('dp', 'ctx')), parts along dimension 0, may hold values from -12 to 12
- keys: bfloat16 [131072, 2048], P(('dp', 'ctx')), parts along dimension 0, may hold values from -12 to 12
- values: bfloat16 [131072, 2048], P(('dp', 'ctx')), parts along dimension 0, may hold values from -6 to 6
- dout: bfloat16 [131072, 2048], P(('dp', 'ctx')), parts along dimension 0, may hold values from -48 to 48
- global_block: int32 [8], P('dp'), parts along dimension 0, may hold values from 0 to 127
Outputs:
- key_grad: bfloat16 [131072, 2048], P(('dp', 'ctx')), parts along dimension 0
- value_grad: bfloat16 [131072, 2048], P(('dp', 'ctx')), parts along dimension 0
The draws below stay inside these ranges and needn't reach their ends.
There are 8 independent parts, one for each index of `dp`. The reference program is written for one: setup_inputs(seed, part) draws one part's arguments, and reference() takes and returns one part's arrays. A program takes and returns all parts, laid end to end along the dimension named above; each array names one. Nothing has to cross between parts.
All inputs are finite; a program needn't handle non-finite values.
Results may differ from the reference program's by a relative error of at most 0.0054.
Values may be sent and summed in bfloat16 or wider, within the bound.
No kernel may reach another device: no remote copies, remote signals or barrier semaphores. Data moves between devices by JAX's collectives and lax.ppermute only.
A program may use at most 64 MiB of HBM per device.

```python
import jax
import jax.numpy as jnp
from jax import lax

HEADS = 16
HEAD_DIM = 128
BLOCK = 128
LEVELS = 2
GLOBALS = 1
BLOCKS = 128
SEQ = 16384


def draw_queries(key, part):
    width = HEADS * HEAD_DIM
    base = jax.random.truncated_normal(jax.random.fold_in(key, 1), -6.0, 6.0, (SEQ, width), jnp.float32)
    return base.astype(jnp.bfloat16)


def draw_keys(key, part):
    width = HEADS * HEAD_DIM
    base = jax.random.truncated_normal(jax.random.fold_in(key, 2), -6.0, 6.0, (SEQ, width), jnp.float32)
    return base.astype(jnp.bfloat16)


def shard_levels(rng, extent, pieces, smallest, high):
    def one(position, parts):
        heights = jax.random.uniform(jax.random.fold_in(jax.random.fold_in(rng, 6), position), (parts,), jnp.float32, smallest / len(pieces), high / len(pieces))
        return jnp.repeat(jnp.exp(heights), extent[position] // parts).reshape((-1,) + (1,) * (len(extent) - position - 1))

    gain = one(*pieces[0])
    for cut in pieces[1:]:
        gain = gain * one(*cut)
    return gain


def gaussian(rng, shape, deviation, reach, cuts=(), held_as=jnp.bfloat16):
    loudness = shard_levels(rng, shape, cuts, -0.22, 0.18) if cuts else 1.0
    entries = jax.random.normal(rng, shape, jnp.float32) * deviation * loudness
    return jnp.minimum(jnp.maximum(entries, -reach), reach).astype(held_as)


def setup_inputs(seed: int = 0, part: int = 0) -> dict:
    streams_of = jax.random.split(jax.random.key(seed), 6)
    part_keys = jax.random.split(jax.random.fold_in(streams_of[5], part), 6)
    queries = draw_queries(jax.random.fold_in(jax.random.fold_in(streams_of[5], part), 71), part)
    keys = draw_keys(jax.random.fold_in(jax.random.fold_in(streams_of[5], part), 71), part)
    values = gaussian(part_keys[2], (SEQ, HEADS * HEAD_DIM), 1.0, 6.0, ((0, 128),))
    dout = gaussian(part_keys[3], (SEQ, HEADS * HEAD_DIM), 8.0, 48.0, ((0, 128),))
    global_block = jax.random.randint(part_keys[4], (GLOBALS,), 0, BLOCKS).astype(jnp.int32)
    return dict(queries=queries, keys=keys, values=values, dout=dout, global_block=global_block)


def round_trip(value):
    return lax.optimization_barrier(value.astype(jnp.bfloat16)).astype(jnp.float32)


def reference(queries, keys, values, dout, global_block):
    head_shape = (BLOCKS, BLOCK, HEADS, HEAD_DIM)
    q_blocks = queries.reshape(head_shape)
    k_blocks = keys.reshape(head_shape)
    v_blocks = values.reshape(head_shape)
    d_blocks = dout.reshape(head_shape)
    inv_root = HEAD_DIM ** -0.5
    block_ids = jnp.arange(BLOCKS, dtype=jnp.int32)

    def key_list(query_block):
        listed = [query_block]
        for section_bit in range(LEVELS):
            listed.append(jnp.bitwise_xor(query_block, 1 << section_bit))
        for slot in range(GLOBALS):
            listed.append(global_block[slot])
        return jnp.stack(listed).astype(jnp.int32)

    def forward_block(query_block):
        listed = key_list(query_block)
        key_rows = k_blocks[listed].reshape(-1, HEADS, HEAD_DIM).astype(jnp.float32)
        value_rows = v_blocks[listed].reshape(-1, HEADS, HEAD_DIM).astype(jnp.float32)
        query_rows = q_blocks[query_block].astype(jnp.float32)
        dout_rows = d_blocks[query_block].astype(jnp.float32)
        logits = jnp.einsum("qhd,khd->hqk", query_rows, key_rows) * inv_root
        row_top = jnp.max(logits, axis=2)
        log_total = row_top + jnp.log(jnp.sum(jnp.exp(logits - row_top[:, :, None]), axis=2))
        prob_full = jnp.exp(logits - log_total[:, :, None])
        prob_grad = jnp.einsum("qhd,khd->hqk", dout_rows, value_rows)
        row_delta = jnp.sum(prob_full * prob_grad, axis=2)
        return log_total, row_delta

    log_totals, row_deltas = lax.map(forward_block, block_ids)

    def contribution(query_block, key_block):
        query_rows = q_blocks[query_block].astype(jnp.float32)
        dout_rows = d_blocks[query_block].astype(jnp.float32)
        key_rows = k_blocks[key_block].astype(jnp.float32)
        value_rows = v_blocks[key_block].astype(jnp.float32)
        logits = jnp.einsum("qhd,khd->hqk", query_rows, key_rows) * inv_root
        prob_full = jnp.exp(logits - log_totals[query_block][:, :, None])
        prob_grad = jnp.einsum("qhd,khd->hqk", dout_rows, value_rows)
        logit_grad = round_trip(prob_full * (prob_grad - row_deltas[query_block][:, :, None]))
        prob_low = round_trip(prob_full)
        key_part = jnp.einsum("hqk,qhd->khd", logit_grad, query_rows) * inv_root
        value_part = jnp.einsum("hqk,qhd->khd", prob_low, dout_rows)
        return key_part, value_part

    global_keys = []
    global_values = []
    for slot in range(GLOBALS):
        def accumulate(carry, query_block, slot=slot):
            part_key, part_value = contribution(query_block, global_block[slot])
            return (carry[0] + part_key, carry[1] + part_value), None

        zeros = jnp.zeros((BLOCK, HEADS, HEAD_DIM), jnp.float32)
        totals, unused = lax.scan(accumulate, (zeros, zeros), block_ids)
        global_keys.append(totals[0])
        global_values.append(totals[1])

    def key_block_grads(key_block):
        key_part, value_part = contribution(key_block, key_block)
        for section_bit in range(LEVELS):
            far_key, far_value = contribution(jnp.bitwise_xor(key_block, 1 << section_bit), key_block)
            key_part = key_part + round_trip(far_key)
            value_part = value_part + round_trip(far_value)
        for slot in range(GLOBALS):
            chosen = key_block == global_block[slot]
            key_part = key_part + jnp.where(chosen, global_keys[slot], jnp.float32(0.0))
            value_part = value_part + jnp.where(chosen, global_values[slot], jnp.float32(0.0))
        return key_part.astype(jnp.bfloat16), value_part.astype(jnp.bfloat16)

    key_grads, value_grads = lax.map(key_block_grads, block_ids)
    flat = (SEQ, HEADS * HEAD_DIM)
    return key_grads.reshape(flat), value_grads.reshape(flat)
```

```python
import jax
import jax.numpy as jnp
from jax import lax
from jax.experimental import pallas as pl
from jax.experimental.pallas import tpu as pltpu
from jax.sharding import PartitionSpec as P

HEADS = 16
HEAD_DIM = 128
BLOCK = 128
LEVELS = 2
WIDTH = HEADS * HEAD_DIM
HEADS_PER_STEP = 4
NEAR = (1, 2, 3, 6)
FAR = (4, 5)
NEAR_COUNT = 1 << len(NEAR)
CHUNK = BLOCK // NEAR_COUNT


def swapped(value, mask):
    pairs = [(source, source ^ mask) for source in range(lax.axis_size("ctx"))]
    return lax.ppermute(value, "ctx", pairs)


def groups(bits):
    spread = [
        sum(((k >> i) & 1) << bit for i, bit in enumerate(bits)) for k in range(1 << len(bits))
    ]
    mask = spread[-1]
    return [
        [base | part for part in spread]
        for base in range(lax.axis_size("ctx"))
        if not base & mask
    ]


def picked(index, bits):
    return sum(((index >> bit) & 1) << i for i, bit in enumerate(bits))


def near_exchange(value):
    return lax.all_to_all(value, "ctx", 0, 0, axis_index_groups=groups(NEAR))


def far_gather(value):
    return lax.all_gather(value, "ctx", axis_index_groups=groups(FAR))


def added(parts):
    terms = [parts[i].astype(jnp.float32) for i in range(parts.shape[0])]
    while len(terms) > 1:
        terms = [a + b for a, b in zip(terms[::2], terms[1::2])]
    return terms[0].astype(jnp.bfloat16)


def near_gather(value):
    copies = jnp.broadcast_to(value[None], (NEAR_COUNT,) + value.shape)
    return near_exchange(copies).reshape(BLOCK, WIDTH)


def attention_kernel(
    core_ref, q_ref, d_ref, k0, k1, k2, ka, v0, v1, v2, va,
    own_k, own_v, b1_k, b1_v, b2_k, b2_v, g_k, g_v,
):
    inv_root = HEAD_DIM ** (-0.5)
    first = core_ref[0] == 0
    last = (((1,), (1,)), ((), ()))
    for h in range(HEADS_PER_STEP):
        cols = pl.ds(h * HEAD_DIM, HEAD_DIM)
        q = q_ref[:, cols]
        d = d_ref[:, cols]
        mine, got = ka[:, cols], va[:, cols]
        key_glob = jnp.where(first, mine, got)
        value_glob = jnp.where(first, got, mine)
        keys = [k0[:, cols], k1[:, cols], k2[:, cols], key_glob]
        values = [v0[:, cols], v1[:, cols], v2[:, cols], value_glob]
        logits = [
            lax.dot_general(k, q, last, preferred_element_type=jnp.float32) * inv_root
            for k in keys
        ]
        top = jnp.max(
            jnp.maximum(jnp.maximum(logits[0], logits[1]), jnp.maximum(logits[2], logits[3])),
            axis=0, keepdims=True,
        )
        exps = [jnp.exp(x - top) for x in logits]
        total = jnp.sum((exps[0] + exps[1]) + (exps[2] + exps[3]), axis=0, keepdims=True)
        scale = 1.0 / total
        probs = [e * scale for e in exps]
        grads = [
            lax.dot_general(v, d, last, preferred_element_type=jnp.float32) for v in values
        ]
        prods = [p * g for p, g in zip(probs, grads)]
        delta = jnp.sum((prods[0] + prods[1]) + (prods[2] + prods[3]), axis=0, keepdims=True)
        outs = ((own_k, own_v), (b1_k, b1_v), (b2_k, b2_v), (g_k, g_v))
        for p, g, (out_k, out_v) in zip(probs, grads, outs):
            low = (p * (g - delta)).astype(jnp.bfloat16)
            key_term = jnp.dot(low, q, preferred_element_type=jnp.float32) * inv_root
            value_term = jnp.dot(
                p.astype(jnp.bfloat16), d, preferred_element_type=jnp.float32
            )
            out_k[:, cols] = key_term.astype(out_k.dtype)
            out_v[:, cols] = value_term.astype(out_v.dtype)


def attention(core, *arrays):
    block = pl.BlockSpec((BLOCK, HEADS_PER_STEP * HEAD_DIM), lambda i: (0, i))
    low = jax.ShapeDtypeStruct((BLOCK, WIDTH), jnp.bfloat16)
    full = jax.ShapeDtypeStruct((BLOCK, WIDTH), jnp.float32)
    return pl.pallas_call(
        attention_kernel,
        grid=(HEADS // HEADS_PER_STEP,),
        in_specs=[pl.BlockSpec(memory_space=pltpu.SMEM)] + [block] * len(arrays),
        out_specs=[block] * 8,
        out_shape=[full, full, low, low, low, low, low, low],
        cost_estimate=pl.CostEstimate(
            flops=2 * 4 * HEADS * BLOCK * 4 * BLOCK * HEAD_DIM,
            bytes_accessed=24 * BLOCK * WIDTH * 2,
            transcendentals=HEADS * BLOCK * 4 * BLOCK,
        ),
        compiler_params=pltpu.CompilerParams(vmem_limit_bytes=32 * 1024 * 1024),
    )(core, *arrays)


def body(queries, keys, values, dout, global_block):
    me = lax.axis_index("ctx")
    root = global_block[0]
    first_core = (me & 1) == 0

    share = jnp.where(first_core, keys, values)
    share_got = swapped(jnp.where(first_core, values, keys), 1)
    rest_got = swapped(share, 1)
    key_1 = jnp.where(first_core, share_got, rest_got)
    value_1 = jnp.where(first_core, rest_got, share_got)
    key_2 = swapped(keys, 2)
    value_2 = swapped(values, 2)

    share = jnp.where(((root ^ me) & 1) == 0, share, share_got)
    chunks = near_exchange(share.reshape(NEAR_COUNT, CHUNK, WIDTH))
    chunk = lax.dynamic_index_in_dim(chunks, picked(root, NEAR), 0, keepdims=False)
    chunk = lax.dynamic_index_in_dim(far_gather(chunk), picked(root, FAR), 0, keepdims=False)
    glob_mine = near_gather(chunk)
    glob_got = swapped(glob_mine, 1)

    core = (me & 1).astype(jnp.int32).reshape(1)
    own_k, own_v, b1_k, b1_v, b2_k, b2_v, g_k, g_v = attention(
        core, queries, dout, keys, key_1, key_2, glob_mine, values, value_1, value_2, glob_got
    )

    part = jnp.where(first_core, g_k, g_v).astype(jnp.float32)
    part = part + swapped(jnp.where(first_core, g_v, g_k), 1).astype(jnp.float32)
    parts = near_exchange(part.astype(jnp.bfloat16).reshape(NEAR_COUNT, CHUNK, WIDTH))
    part = added(far_gather(added(parts)))
    total_mine = near_gather(part)
    total_got = swapped(total_mine, 1)
    total_k = jnp.where(first_core, total_mine, total_got)
    total_v = jnp.where(first_core, total_got, total_mine)

    back_1k, back_1v = swapped((b1_k, b1_v), 1)
    back_2k, back_2v = swapped((b2_k, b2_v), 2)
    chosen = me == root

    def final(own, back_1, back_2, total):
        out = own + back_1.astype(jnp.float32) + back_2.astype(jnp.float32)
        out = out + jnp.where(chosen, total.astype(jnp.float32), jnp.float32(0.0))
        return out.astype(jnp.bfloat16)

    return final(own_k, back_1k, back_2k, total_k), final(own_v, back_1v, back_2v, total_v)


def solution(mesh):
    rows = P(("dp", "ctx"), None)
    return jax.shard_map(
        body,
        mesh=mesh,
        in_specs=(rows, rows, rows, rows, P("dp")),
        out_specs=(rows, rows),
        check_vma=False,
    )
```

```python
import jax
import jax.numpy as jnp
from jax import lax
from jax.experimental import pallas as pl
from jax.experimental.pallas import tpu as pltpu
from jax.sharding import PartitionSpec as P

HEADS = 16
HEAD_DIM = 128
BLOCK = 128
LEVELS = 2
WIDTH = HEADS * HEAD_DIM
INV_ROOT = HEAD_DIM ** (-0.5)
STEP_HEADS = 4
STEPS = HEADS // STEP_HEADS
STEP_COLS = STEP_HEADS * HEAD_DIM
STAT_ROWS = 8
TEAM = (0, 1, 2, 6)
QUAD = 4
PAIR_BIT = 3
FAR = (4, 5)
LAST = (((1,), (1,)), ((), ()))


def swapped(value, mask):
    pairs = [(source, source ^ mask) for source in range(lax.axis_size("ctx"))]
    return lax.ppermute(value, "ctx", pairs)


def groups(bits):
    spread = [
        sum(((k >> i) & 1) << bit for i, bit in enumerate(bits)) for k in range(1 << len(bits))
    ]
    mask = spread[-1]
    return [
        [base | part for part in spread]
        for base in range(lax.axis_size("ctx"))
        if not base & mask
    ]


def picked(parts, root, bits):
    index = sum(((root >> bit) & 1) << i for i, bit in enumerate(bits))
    return lax.dynamic_index_in_dim(parts, index, 0, keepdims=False)


def exchange(value, bits):
    return lax.all_to_all(value, "ctx", 0, 0, axis_index_groups=groups(bits))


def far_gather(value):
    return lax.all_gather(value, "ctx", axis_index_groups=groups(FAR))


def added(parts):
    terms = [parts[i].astype(jnp.float32) for i in range(parts.shape[0])]
    while len(terms) > 1:
        terms = [a + b for a, b in zip(terms[::2], terms[1::2])]
    return terms[0].astype(jnp.bfloat16)


def dot_last(a, b):
    return lax.dot_general(a, b, LAST, preferred_element_type=jnp.float32)


def dot(a, b):
    return jnp.dot(a, b, preferred_element_type=jnp.float32)


def sum_rows(value):
    return jnp.sum(value, axis=0, keepdims=True)


def max_rows(value):
    return jnp.max(value, axis=0, keepdims=True)


def cost(dots, exps, size):
    return pl.CostEstimate(
        flops=2 * dots * BLOCK * BLOCK * HEAD_DIM,
        transcendentals=exps * BLOCK * BLOCK,
        bytes_accessed=size * BLOCK * HEAD_DIM * 2,
    )


PARAMS = pltpu.CompilerParams(vmem_limit_bytes=32 * 1024 * 1024)
SCALARS = pl.BlockSpec(memory_space=pltpu.SMEM)
COLS = pl.BlockSpec((BLOCK, QUAD * HEAD_DIM), lambda i: (0, i))
TILES = pl.BlockSpec((QUAD, 2, BLOCK, HEAD_DIM), lambda i: (i, 0, 0, 0))
STATS = pl.BlockSpec((QUAD, STAT_ROWS, BLOCK), lambda i: (i, 0, 0))
WHOLE = pl.BlockSpec(memory_space=pltpu.VMEM)
ROWS_SHAPE = jax.ShapeDtypeStruct((BLOCK, WIDTH), jnp.bfloat16)
TILES_SHAPE = jax.ShapeDtypeStruct((HEADS, 2, BLOCK, HEAD_DIM), jnp.bfloat16)
STATS_SHAPE = jax.ShapeDtypeStruct((HEADS, STAT_ROWS, BLOCK), jnp.float32)
PAIR_SHAPE = jax.ShapeDtypeStruct((2, BLOCK, HEAD_DIM), jnp.float32)


def head(h):
    return pl.ds(h * HEAD_DIM, HEAD_DIM)


def split_kernel(a_ref, b_ref, out_ref):
    for h in range(QUAD):
        out_ref[h, 0] = a_ref[:, head(h)]
        out_ref[h, 1] = b_ref[:, head(h)]


def split_heads(a, b):
    return pl.pallas_call(
        split_kernel,
        grid=(HEADS // QUAD,),
        in_specs=[COLS, COLS],
        out_specs=TILES,
        out_shape=TILES_SHAPE,
        cost_estimate=cost(0, 0, 64),
        compiler_params=PARAMS,
    )(a, b)


def merge_kernel(tiles_ref, a_ref, b_ref):
    for h in range(QUAD):
        a_ref[:, head(h)] = tiles_ref[h, 0]
        b_ref[:, head(h)] = tiles_ref[h, 1]


def merge_heads(tiles):
    return pl.pallas_call(
        merge_kernel,
        grid=(HEADS // QUAD,),
        in_specs=[TILES],
        out_specs=[COLS, COLS],
        out_shape=[ROWS_SHAPE, ROWS_SHAPE],
        cost_estimate=cost(0, 0, 64),
        compiler_params=PARAMS,
    )(tiles)


def local_stats_kernel(qd_ref, kv_ref, out_ref):
    for b in range(QUAD):
        q, d = qd_ref[b, 0], qd_ref[b, 1]
        near = (b, b ^ 1, b ^ 2)
        logits = [dot_last(kv_ref[c, 0], q) * INV_ROOT for c in near]
        top = max_rows(jnp.maximum(jnp.maximum(logits[0], logits[1]), logits[2]))
        exps = [jnp.exp(x - top) for x in logits]
        grads = [dot_last(kv_ref[c, 1], d) for c in near]
        out_ref[b, 0:1] = top
        out_ref[b, 1:2] = sum_rows(exps[0] + exps[1] + exps[2])
        out_ref[b, 2:3] = sum_rows(exps[0] * grads[0] + exps[1] * grads[1] + exps[2] * grads[2])
        out_ref[b, 3:8] = jnp.zeros((STAT_ROWS - 3, BLOCK), jnp.float32)


def local_stats(qd, kv):
    return pl.pallas_call(
        local_stats_kernel,
        grid=(HEADS // QUAD,),
        in_specs=[TILES, TILES],
        out_specs=STATS,
        out_shape=STATS_SHAPE,
        cost_estimate=cost(96, 48, 70),
        compiler_params=PARAMS,
    )(qd, kv)


def global_kernel(flags_ref, qd_ref, mine_ref, got_ref, stats_ref, sum_ref, out_ref):
    keys_mine = flags_ref[0] == 0
    key = jnp.where(keys_mine, mine_ref[...], got_ref[...])
    value = jnp.where(keys_mine, got_ref[...], mine_ref[...])
    key_sum = jnp.zeros((BLOCK, HEAD_DIM), jnp.float32)
    value_sum = jnp.zeros((BLOCK, HEAD_DIM), jnp.float32)
    for b in range(HEADS):
        q, d = qd_ref[b, 0], qd_ref[b, 1]
        logits = dot_last(key, q) * INV_ROOT
        grad = dot_last(value, d)
        local_top = stats_ref[b, 0:1]
        top = jnp.maximum(local_top, max_rows(logits))
        fade = jnp.exp(local_top - top)
        exps = jnp.exp(logits - top)
        scale = 1.0 / (stats_ref[b, 1:2] * fade + sum_rows(exps))
        delta = (stats_ref[b, 2:3] * fade + sum_rows(exps * grad)) * scale
        prob = exps * scale
        key_sum += dot((prob * (grad - delta)).astype(jnp.bfloat16), q)
        value_sum += dot(prob.astype(jnp.bfloat16), d)
        out_ref[b, 0:1] = top
        out_ref[b, 1:2] = scale
        out_ref[b, 2:3] = delta
        out_ref[b, 3:8] = jnp.zeros((STAT_ROWS - 3, BLOCK), jnp.float32)
    sum_ref[0] = key_sum * INV_ROOT
    sum_ref[1] = value_sum


def global_terms(flags, *arrays):
    return pl.pallas_call(
        global_kernel,
        in_specs=[SCALARS] + [WHOLE] * 4,
        out_specs=[WHOLE] * 2,
        out_shape=[PAIR_SHAPE, STATS_SHAPE],
        cost_estimate=cost(64, 16, 80),
        compiler_params=PARAMS,
    )(flags, *arrays)


def local_terms_kernel(flags_ref, qd_ref, kv_ref, stats_ref, out_ref, root_ref):
    step = pl.program_id(0)

    @pl.when(step == 0)
    def _():
        root_ref[...] = jnp.zeros_like(root_ref)

    for c in range(QUAD):
        k, v = kv_ref[c, 0], kv_ref[c, 1]
        key_sum = value_sum = None
        for a in (c, c ^ 1, c ^ 2):
            q, d = qd_ref[a, 0], qd_ref[a, 1]
            top, scale, delta = (stats_ref[a, i : i + 1] for i in range(3))
            prob = jnp.exp(dot_last(k, q) * INV_ROOT - top) * scale
            grad = dot_last(v, d)
            key_term = dot((prob * (grad - delta)).astype(jnp.bfloat16), q) * INV_ROOT
            value_term = dot(prob.astype(jnp.bfloat16), d)
            if a == c:
                key_sum, value_sum = key_term, value_term
            else:
                key_sum += key_term.astype(jnp.bfloat16).astype(jnp.float32)
                value_sum += value_term.astype(jnp.bfloat16).astype(jnp.float32)
        out_ref[c, 0] = key_sum.astype(jnp.bfloat16)
        out_ref[c, 1] = value_sum.astype(jnp.bfloat16)

        @pl.when(flags_ref[1] == step * QUAD + c)
        def _():
            root_ref[0] = key_sum
            root_ref[1] = value_sum


def local_terms(flags, *arrays):
    return pl.pallas_call(
        local_terms_kernel,
        grid=(HEADS // QUAD,),
        in_specs=[SCALARS, TILES, TILES, STATS],
        out_specs=[TILES, pl.BlockSpec((2, BLOCK, HEAD_DIM), lambda i: (0, 0, 0))],
        out_shape=[TILES_SHAPE, PAIR_SHAPE],
        cost_estimate=cost(192, 48, 100),
        compiler_params=PARAMS,
    )(flags, *arrays)


def body(queries, keys, values, dout, global_block):
    me = lax.axis_index("ctx")
    root = global_block[0]
    kind = (me >> PAIR_BIT) & 1
    keys_mine = kind == 0
    root_index = sum(((root >> bit) & 1) << i for i, bit in enumerate(TEAM))
    team_mask = sum(1 << bit for bit in TEAM)
    root_here = (root | team_mask) == (me | team_mask)
    flags = jnp.stack([kind, root_index]).astype(jnp.int32)

    kv = exchange(split_heads(keys, values), TEAM)
    qd, kv = lax.optimization_barrier((split_heads(queries, dout), kv))
    qd = exchange(qd, TEAM)

    held = lax.dynamic_index_in_dim(kv, root_index, 0, keepdims=False)
    got = swapped(jnp.where(keys_mine, held[1], held[0]), 1 << PAIR_BIT)
    root_kind = (root >> PAIR_BIT) & 1
    mine = jnp.where(root_kind == kind, jnp.where(keys_mine, held[0], held[1]), got)
    mine = picked(far_gather(mine), root, FAR)
    got = swapped(mine, 1 << PAIR_BIT)

    stats = local_stats(qd, kv)
    sums, stats = global_terms(flags, qd, mine, got, stats)

    send = jnp.where(keys_mine, sums[1], sums[0]).astype(jnp.bfloat16)
    part = jnp.where(keys_mine, sums[0], sums[1])
    part = part + swapped(send, 1 << PAIR_BIT).astype(jnp.float32)
    mine = added(far_gather(part.astype(jnp.bfloat16)))
    got = swapped(mine, 1 << PAIR_BIT)
    total = jnp.stack([jnp.where(keys_mine, mine, got), jnp.where(keys_mine, got, mine)])

    grads, root_grads = local_terms(flags, qd, kv, stats)
    root_grads = root_grads + jnp.where(root_here, total.astype(jnp.float32), 0.0)
    grads = lax.dynamic_update_index_in_dim(
        grads, root_grads.astype(jnp.bfloat16), root_index, 0
    )
    return tuple(merge_heads(exchange(grads, TEAM)))


def solution(mesh):
    rows = P(("dp", "ctx"), None)
    return jax.shard_map(
        body,
        mesh=mesh,
        in_specs=(rows, rows, rows, rows, P("dp")),
        out_specs=(rows, rows),
        check_vma=False,
    )
```

```python
import functools

import jax
import jax.numpy as jnp
from jax import lax
from jax.experimental import pallas as pl
from jax.experimental.pallas import tpu as pltpu
from jax.sharding import PartitionSpec as P

HEADS = 16
HEAD_DIM = 128
BLOCK = 128
LEVELS = 2
WIDTH = HEADS * HEAD_DIM
INV_ROOT = HEAD_DIM ** (-0.5)
STEP_HEADS = 4
STEPS = HEADS // STEP_HEADS
STEP_COLS = STEP_HEADS * HEAD_DIM
STAT_ROWS = 8
TEAM = (0, 1, 6)
QUAD = 4
TEAM_SIZE = 8
TEAM_HEADS = 2
NEAR = (2, 3)
FAR = (4, 5)
LAST = (((1,), (1,)), ((), ()))


def groups(bits):
    spread = [
        sum(((k >> i) & 1) << bit for i, bit in enumerate(bits)) for k in range(1 << len(bits))
    ]
    mask = spread[-1]
    return [
        [base | part for part in spread]
        for base in range(lax.axis_size("ctx"))
        if not base & mask
    ]


def picked(root, bits):
    index = sum(((root >> bit) & 1) << i for i, bit in enumerate(bits))
    return index.astype(jnp.int32).reshape(1)


def exchange(value, bits):
    return lax.all_to_all(value, "ctx", 0, 0, axis_index_groups=groups(bits))


def sent(value, bits, source, target):
    spread_out = [
        sum(((k >> i) & 1) << bit for i, bit in enumerate(bits)) for k in range(1 << len(bits))
    ]
    pairs = [
        (base | spread_out[source], base | spread_out[target])
        for base in range(lax.axis_size("ctx"))
        if not base & spread_out[-1]
    ]
    return lax.ppermute(value, "ctx", pairs)


def by_root(root, bits, branch, *operands):
    branches = [functools.partial(branch, k) for k in range(1 << len(bits))]
    return lax.switch(picked(root, bits)[0], branches, *operands)


def dot_last(a, b):
    return lax.dot_general(a, b, LAST, preferred_element_type=jnp.float32)


def dot(a, b):
    return jnp.dot(a, b, preferred_element_type=jnp.float32)


def sum_rows(value):
    return jnp.sum(value, axis=0, keepdims=True)


def max_rows(value):
    return jnp.max(value, axis=0, keepdims=True)


def cost(dots, exps, size):
    return pl.CostEstimate(
        flops=2 * dots * BLOCK * BLOCK * HEAD_DIM,
        transcendentals=exps * BLOCK * BLOCK,
        bytes_accessed=size * BLOCK * HEAD_DIM * 2,
    )


PARAMS = pltpu.CompilerParams(vmem_limit_bytes=32 * 1024 * 1024)
FULL_PARAMS = pltpu.CompilerParams(vmem_limit_bytes=60 * 1024 * 1024)
SCALARS = pl.BlockSpec(memory_space=pltpu.SMEM)
COLS = pl.BlockSpec((BLOCK, QUAD * HEAD_DIM), lambda i: (0, i))
WHOLE = pl.BlockSpec(memory_space=pltpu.VMEM)
SQUARE = (BLOCK, HEAD_DIM)
LOW, FULL = jnp.bfloat16, jnp.float32
KINDS = 4
PARTS = 2 * TEAM_HEADS
STATS_SHAPE = (TEAM_HEADS, TEAM_SIZE, STAT_ROWS, BLOCK)


def shaped(shape, dtype):
    return jax.ShapeDtypeStruct(shape, dtype)


def head(h):
    return pl.ds(h * HEAD_DIM, HEAD_DIM)


def split_kernel(*refs):
    for kind, ref in enumerate(refs[:KINDS]):
        for h in range(QUAD):
            refs[-1][h, kind] = ref[:, head(h)]


def split_heads(*arrays):
    return pl.pallas_call(
        split_kernel,
        grid=(HEADS // QUAD,),
        in_specs=[COLS] * KINDS,
        out_specs=pl.BlockSpec((QUAD, KINDS) + SQUARE, lambda i: (i, 0, 0, 0)),
        out_shape=shaped((HEADS, KINDS) + SQUARE, LOW),
        cost_estimate=cost(0, 0, 128),
        compiler_params=FULL_PARAMS,
    )(*arrays)


def merge_kernel(tiles_ref, a_ref, b_ref):
    for h in range(QUAD):
        a_ref[:, head(h)] = tiles_ref[h, 0]
        b_ref[:, head(h)] = tiles_ref[h, 1]


def merge_heads(tiles):
    return pl.pallas_call(
        merge_kernel,
        grid=(HEADS // QUAD,),
        in_specs=[pl.BlockSpec((QUAD, 2) + SQUARE, lambda i: (i, 0, 0, 0))],
        out_specs=[COLS, COLS],
        out_shape=[shaped((BLOCK, WIDTH), LOW)] * 2,
        cost_estimate=cost(0, 0, 64),
        compiler_params=PARAMS,
    )(tiles)


def spread_kernel(index_ref, *refs):
    out_ref = refs[-1]
    for i, ref in enumerate(refs[:-1]):

        @pl.when(index_ref[0] == i)
        def _(ref=ref):
            for j in range(out_ref.shape[0]):
                out_ref[j] = ref[...]


def spread(copies, index, *arrays):
    return pl.pallas_call(
        spread_kernel,
        in_specs=[SCALARS] + [WHOLE] * len(arrays),
        out_specs=WHOLE,
        out_shape=shaped((copies,) + SQUARE, LOW),
        cost_estimate=cost(0, 0, 8),
        compiler_params=PARAMS,
    )(index, *arrays)


def added(arrays):
    a, b, c, d = (x.astype(FULL) for x in arrays)
    return ((a + b) + (c + d)).astype(LOW)


def local_stats_kernel(team_ref, out_ref):
    for b in range(QUAD):
        q, d = team_ref[b, 2], team_ref[b, 3]
        near = (b, b ^ 1, b ^ 2)
        logits = [dot_last(team_ref[c, 0], q) * INV_ROOT for c in near]
        top = max_rows(jnp.maximum(jnp.maximum(logits[0], logits[1]), logits[2]))
        exps = [jnp.exp(x - top) for x in logits]
        grads = [dot_last(team_ref[c, 1], d) for c in near]
        out_ref[0, b, 0:1] = top
        out_ref[0, b, 1:2] = sum_rows(exps[0] + exps[1] + exps[2])
        out_ref[0, b, 2:3] = sum_rows(exps[0] * grads[0] + exps[1] * grads[1] + exps[2] * grads[2])
        out_ref[0, b, 3:8] = jnp.zeros((STAT_ROWS - 3, BLOCK), jnp.float32)


def local_stats(team):
    return pl.pallas_call(
        local_stats_kernel,
        grid=(TEAM_SIZE // QUAD, TEAM_HEADS),
        in_specs=[pl.BlockSpec((QUAD, KINDS) + SQUARE, lambda i, j: (i, j, 0, 0))],
        out_specs=pl.BlockSpec((1, QUAD, STAT_ROWS, BLOCK), lambda i, j: (j, i, 0, 0)),
        out_shape=shaped(STATS_SHAPE, FULL),
        cost_estimate=cost(96, 48, 70),
        compiler_params=PARAMS,
    )(team)


def global_kernel(team_ref, kv_ref, stats_ref, sum_ref, out_ref):
    for j in range(TEAM_HEADS):
        key, value = kv_ref[2 * j], kv_ref[2 * j + 1]
        key_sum = jnp.zeros((BLOCK, HEAD_DIM), jnp.float32)
        value_sum = jnp.zeros((BLOCK, HEAD_DIM), jnp.float32)
        for b in range(TEAM_SIZE):
            q, d = team_ref[b, KINDS * j + 2], team_ref[b, KINDS * j + 3]
            logits = dot_last(key, q) * INV_ROOT
            grad = dot_last(value, d)
            local_top = stats_ref[j, b, 0:1]
            top = jnp.maximum(local_top, max_rows(logits))
            fade = jnp.exp(local_top - top)
            exps = jnp.exp(logits - top)
            scale = 1.0 / (stats_ref[j, b, 1:2] * fade + sum_rows(exps))
            delta = (stats_ref[j, b, 2:3] * fade + sum_rows(exps * grad)) * scale
            prob = exps * scale
            key_sum += dot((prob * (grad - delta)).astype(jnp.bfloat16), q)
            value_sum += dot(prob.astype(jnp.bfloat16), d)
            out_ref[j, b, 0:1] = top
            out_ref[j, b, 1:2] = scale
            out_ref[j, b, 2:3] = delta
            out_ref[j, b, 3:8] = jnp.zeros((STAT_ROWS - 3, BLOCK), jnp.float32)
        sum_ref[2 * j] = (key_sum * INV_ROOT).astype(sum_ref.dtype)
        sum_ref[2 * j + 1] = value_sum.astype(sum_ref.dtype)


def global_terms(*arrays):
    return pl.pallas_call(
        global_kernel,
        in_specs=[WHOLE] * 3,
        out_specs=[WHOLE] * 2,
        out_shape=[shaped((PARTS,) + SQUARE, LOW), shaped(STATS_SHAPE, FULL)],
        cost_estimate=cost(64, 16, 80),
        compiler_params=PARAMS,
    )(*arrays)


def local_terms_kernel(root_ref, team_ref, stats_ref, out_ref, sums_ref):
    quad = pl.program_id(1)
    for c in range(QUAD):
        k, v = team_ref[c, 0], team_ref[c, 1]
        key_sum = value_sum = None
        for a in (c, c ^ 1, c ^ 2):
            q, d = team_ref[a, 2], team_ref[a, 3]
            top, scale, delta = (stats_ref[0, a, i : i + 1] for i in range(3))
            prob = jnp.exp(dot_last(k, q) * INV_ROOT - top) * scale
            grad = dot_last(v, d)
            key_term = dot((prob * (grad - delta)).astype(jnp.bfloat16), q) * INV_ROOT
            value_term = dot(prob.astype(jnp.bfloat16), d)
            if a == c:
                key_sum, value_sum = key_term, value_term
            else:
                key_sum += key_term.astype(jnp.bfloat16).astype(jnp.float32)
                value_sum += value_term.astype(jnp.bfloat16).astype(jnp.float32)
        out_ref[c, 0] = key_sum.astype(jnp.bfloat16)
        out_ref[c, 1] = value_sum.astype(jnp.bfloat16)

        @pl.when(root_ref[0] == quad * QUAD + c)
        def _():
            sums_ref[0] = key_sum
            sums_ref[1] = value_sum


def local_terms(root_index, team, stats):
    return pl.pallas_call(
        local_terms_kernel,
        grid=(TEAM_HEADS, TEAM_SIZE // QUAD),
        in_specs=[
            SCALARS,
            pl.BlockSpec((QUAD, KINDS) + SQUARE, lambda j, i: (i, j, 0, 0)),
            pl.BlockSpec((1, QUAD, STAT_ROWS, BLOCK), lambda j, i: (j, i, 0, 0)),
        ],
        out_specs=[
            pl.BlockSpec((QUAD, 2) + SQUARE, lambda j, i: (i, j, 0, 0)),
            pl.BlockSpec((2,) + SQUARE, lambda j, i: (j, 0, 0)),
        ],
        out_shape=[shaped((TEAM_SIZE, PARTS) + SQUARE, LOW), shaped((PARTS,) + SQUARE, FULL)],
        cost_estimate=cost(192, 48, 100),
        compiler_params=PARAMS,
    )(root_index, team, stats)


def root_kernel(index_ref, here_ref, grads_ref, sums_ref, *refs):
    out_ref = refs[-1]
    for part, ref in enumerate(refs[:-1]):
        whole = (sums_ref[part] + ref[...].astype(FULL)).astype(LOW)
        out_ref[0, part] = jnp.where(here_ref[0] == 1, whole, grads_ref[0, part])


def add_root(index, here, grads, sums, *totals):
    block = pl.BlockSpec((1, PARTS) + SQUARE, lambda i, index_ref, here_ref: (index_ref[0], 0, 0, 0))
    whole = pl.BlockSpec((PARTS,) + SQUARE, lambda i, index_ref, here_ref: (0, 0, 0))
    square = pl.BlockSpec(SQUARE, lambda i, index_ref, here_ref: (0, 0))
    return pl.pallas_call(
        root_kernel,
        grid_spec=pltpu.PrefetchScalarGridSpec(
            num_scalar_prefetch=2,
            grid=(1,),
            in_specs=[block, whole] + [square] * len(totals),
            out_specs=block,
        ),
        out_shape=shaped(grads.shape, LOW),
        input_output_aliases={2: 0},
        cost_estimate=cost(0, 0, 28),
        compiler_params=PARAMS,
    )(index, here, grads, sums, *totals)


def body(queries, keys, values, dout, global_block):
    me = lax.axis_index("ctx")
    root = global_block[0]
    index = picked(root, TEAM)
    near, far = picked(me, NEAR), picked(me, FAR)
    team_mask = sum(1 << bit for bit in TEAM)
    here = ((root | team_mask) == (me | team_mask)).astype(jnp.int32).reshape(1)
    groups_near, groups_far = 1 << len(NEAR), 1 << len(FAR)

    def others(count, k):
        return [i for i in range(count) if i != k]

    def scatter_near(k, *parts):
        got = list(parts)
        for i in others(groups_near, k):
            got[i] = sent(parts[i], NEAR, k, i)
        return spread(1, near, *got)[0]

    def send_far(k, part):
        got = [part] * groups_far
        for i in others(groups_far, k):
            got[i] = sent(part, FAR, k, i)
        return spread(groups_near, far, *got)

    def sum_far(k, part, team, stats):
        got = [part] + [sent(part, FAR, i, k) for i in others(groups_far, k)]
        return (added(got),) + tuple(local_terms(index, team, stats))

    def gather_near(k, part):
        got = [part] * groups_near
        for i in others(groups_near, k):
            got[i] = sent(part, NEAR, i, k)
        return tuple(got)

    team = split_heads(keys, values, queries, dout)
    team = exchange(team.reshape((TEAM_SIZE, TEAM_HEADS * KINDS) + SQUARE), TEAM)

    held = lax.dynamic_index_in_dim(team, index[0], 0, keepdims=False)
    part = by_root(root, NEAR, scatter_near, *(held[i] for i in (0, 1, KINDS, KINDS + 1)))
    glob = exchange(by_root(root, FAR, send_far, part), NEAR)
    sums, stats = global_terms(team, glob, local_stats(team))

    part = added(exchange(sums, NEAR))
    part, grads, local_sums = by_root(root, FAR, sum_far, part, team, stats)
    totals = by_root(root, NEAR, gather_near, part)

    grads = exchange(add_root(index, here, grads, local_sums, *totals), TEAM)
    return tuple(merge_heads(grads.reshape((HEADS, 2) + SQUARE)))


def solution(mesh):
    rows = P(("dp", "ctx"), None)
    return jax.shard_map(
        body,
        mesh=mesh,
        in_specs=(rows, rows, rows, rows, P("dp")),
        out_specs=(rows, rows),
        check_vma=False,
    )
```

```python
import functools

import jax
import jax.numpy as jnp
from jax import lax
from jax.experimental import pallas as pl
from jax.experimental.pallas import tpu as pltpu
from jax.sharding import PartitionSpec as P

HEADS = 16
HEAD_DIM = 128
BLOCK = 128
LEVELS = 2
WIDTH = HEADS * HEAD_DIM
INV_ROOT = HEAD_DIM ** (-0.5)
STEP_HEADS = 4
STEPS = HEADS // STEP_HEADS
STEP_COLS = STEP_HEADS * HEAD_DIM
STAT_ROWS = 8
TEAM = (0, 1, 6)
QUAD = 4
TEAM_SIZE = 8
TEAM_HEADS = 2
NEAR = (2, 3)
FAR = (4, 5)
LAST = (((1,), (1,)), ((), ()))


def groups(bits):
    spread = [
        sum(((k >> i) & 1) << bit for i, bit in enumerate(bits)) for k in range(1 << len(bits))
    ]
    mask = spread[-1]
    return [
        [base | part for part in spread]
        for base in range(lax.axis_size("ctx"))
        if not base & mask
    ]


def picked(root, bits):
    index = sum(((root >> bit) & 1) << i for i, bit in enumerate(bits))
    return index.astype(jnp.int32).reshape(1)


def exchange(value, bits):
    return lax.all_to_all(value, "ctx", 0, 0, axis_index_groups=groups(bits))


def sent(value, bits, source, target):
    spread_out = [
        sum(((k >> i) & 1) << bit for i, bit in enumerate(bits)) for k in range(1 << len(bits))
    ]
    pairs = [
        (base | spread_out[source], base | spread_out[target])
        for base in range(lax.axis_size("ctx"))
        if not base & spread_out[-1]
    ]
    return lax.ppermute(value, "ctx", pairs)


def by_root(root, bits, branch, *operands):
    branches = [functools.partial(branch, k) for k in range(1 << len(bits))]
    return lax.switch(picked(root, bits)[0], branches, *operands)


def dot_last(a, b):
    return lax.dot_general(a, b, LAST, preferred_element_type=jnp.float32)


def dot(a, b):
    return jnp.dot(a, b, preferred_element_type=jnp.float32)


def sum_rows(value):
    return jnp.sum(value, axis=0, keepdims=True)


def max_rows(value):
    return jnp.max(value, axis=0, keepdims=True)


def cost(dots, exps, size):
    return pl.CostEstimate(
        flops=2 * dots * BLOCK * BLOCK * HEAD_DIM,
        transcendentals=exps * BLOCK * BLOCK,
        bytes_accessed=size * BLOCK * HEAD_DIM * 2,
    )


PARAMS = pltpu.CompilerParams(vmem_limit_bytes=32 * 1024 * 1024)
FULL_PARAMS = pltpu.CompilerParams(vmem_limit_bytes=60 * 1024 * 1024)
SCALARS = pl.BlockSpec(memory_space=pltpu.SMEM)
STEP_HEADS = 8
COLS = pl.BlockSpec((BLOCK, STEP_HEADS * HEAD_DIM), lambda i: (0, i))
WHOLE = pl.BlockSpec(memory_space=pltpu.VMEM)
SQUARE = (BLOCK, HEAD_DIM)
LOW, FULL = jnp.bfloat16, jnp.float32
KINDS = 4
PARTS = 2 * TEAM_HEADS
TEAM_ROWS = TEAM_SIZE * BLOCK
STATS_SHAPE = (TEAM_HEADS, STAT_ROWS, TEAM_ROWS)


def shaped(shape, dtype):
    return jax.ShapeDtypeStruct(shape, dtype)


def head(h):
    return pl.ds(h * HEAD_DIM, HEAD_DIM)


def split_kernel(*refs):
    for kind, ref in enumerate(refs[:KINDS]):
        for h in range(STEP_HEADS):
            refs[-1][h, kind] = ref[:, head(h)]


def split_heads(*arrays):
    return pl.pallas_call(
        split_kernel,
        grid=(HEADS // STEP_HEADS,),
        in_specs=[COLS] * KINDS,
        out_specs=pl.BlockSpec((STEP_HEADS, KINDS) + SQUARE, lambda i: (i, 0, 0, 0)),
        out_shape=shaped((HEADS, KINDS) + SQUARE, LOW),
        cost_estimate=cost(0, 0, 128),
        compiler_params=FULL_PARAMS,
    )(*arrays)


def merge_kernel(tiles_ref, a_ref, b_ref):
    for h in range(STEP_HEADS):
        a_ref[:, head(h)] = tiles_ref[h, 0]
        b_ref[:, head(h)] = tiles_ref[h, 1]


def merge_heads(tiles):
    return pl.pallas_call(
        merge_kernel,
        grid=(HEADS // STEP_HEADS,),
        in_specs=[pl.BlockSpec((STEP_HEADS, 2) + SQUARE, lambda i: (i, 0, 0, 0))],
        out_specs=[COLS, COLS],
        out_shape=[shaped((BLOCK, WIDTH), LOW)] * 2,
        cost_estimate=cost(0, 0, 64),
        compiler_params=PARAMS,
    )(tiles)


def spread_kernel(index_ref, *refs):
    out_ref = refs[-1]
    for i, ref in enumerate(refs[:-1]):

        @pl.when(index_ref[0] == i)
        def _(ref=ref):
            for j in range(out_ref.shape[0]):
                out_ref[j] = ref[...]


def spread(copies, index, *arrays):
    return pl.pallas_call(
        spread_kernel,
        in_specs=[SCALARS] + [WHOLE] * len(arrays),
        out_specs=WHOLE,
        out_shape=shaped((copies,) + SQUARE, LOW),
        cost_estimate=cost(0, 0, 8),
        compiler_params=PARAMS,
    )(index, *arrays)


def added(arrays):
    a, b, c, d = (x.astype(FULL) for x in arrays)
    return ((a + b) + (c + d)).astype(LOW)


def local_stats_kernel(team_ref, out_ref):
    for b in range(QUAD):
        q, d = team_ref[b, 2], team_ref[b, 3]
        near = (b, b ^ 1, b ^ 2)
        logits = [dot_last(team_ref[c, 0], q) * INV_ROOT for c in near]
        top = max_rows(jnp.maximum(jnp.maximum(logits[0], logits[1]), logits[2]))
        exps = [jnp.exp(x - top) for x in logits]
        grads = [dot_last(team_ref[c, 1], d) for c in near]
        row = head(b)
        out_ref[0, 0:1, row] = top
        out_ref[0, 1:2, row] = sum_rows(exps[0] + exps[1] + exps[2])
        out_ref[0, 2:3, row] = sum_rows(exps[0] * grads[0] + exps[1] * grads[1] + exps[2] * grads[2])
        out_ref[0, 3:8, row] = jnp.zeros((STAT_ROWS - 3, BLOCK), FULL)


def local_stats(team):
    return pl.pallas_call(
        local_stats_kernel,
        grid=(TEAM_SIZE // QUAD, TEAM_HEADS),
        in_specs=[pl.BlockSpec((QUAD, KINDS) + SQUARE, lambda i, j: (i, j, 0, 0))],
        out_specs=pl.BlockSpec((1, STAT_ROWS, QUAD * BLOCK), lambda i, j: (j, 0, i)),
        out_shape=shaped(STATS_SHAPE, FULL),
        cost_estimate=cost(96, 48, 70),
        compiler_params=PARAMS,
    )(team)


def global_kernel(team_ref, kv_ref, stats_ref, sum_ref, out_ref):
    for j in range(TEAM_HEADS):
        q = team_ref[:, KINDS * j + 2].reshape(TEAM_ROWS, HEAD_DIM)
        d = team_ref[:, KINDS * j + 3].reshape(TEAM_ROWS, HEAD_DIM)
        logits = dot_last(kv_ref[2 * j], q) * INV_ROOT
        grad = dot_last(kv_ref[2 * j + 1], d)
        local_top = stats_ref[j, 0:1]
        top = jnp.maximum(local_top, max_rows(logits))
        fade = jnp.exp(local_top - top)
        exps = jnp.exp(logits - top)
        scale = 1.0 / (stats_ref[j, 1:2] * fade + sum_rows(exps))
        delta = (stats_ref[j, 2:3] * fade + sum_rows(exps * grad)) * scale
        prob = exps * scale
        key_sum = dot((prob * (grad - delta)).astype(LOW), q) * INV_ROOT
        sum_ref[2 * j] = key_sum.astype(sum_ref.dtype)
        sum_ref[2 * j + 1] = dot(prob.astype(LOW), d).astype(sum_ref.dtype)
        out_ref[j, 0:1] = top
        out_ref[j, 1:2] = scale
        out_ref[j, 2:3] = delta
        out_ref[j, 3:8] = jnp.zeros((STAT_ROWS - 3, TEAM_ROWS), FULL)


def global_terms(*arrays):
    return pl.pallas_call(
        global_kernel,
        in_specs=[WHOLE] * 3,
        out_specs=[WHOLE] * 2,
        out_shape=[shaped((PARTS,) + SQUARE, LOW), shaped(STATS_SHAPE, FULL)],
        cost_estimate=cost(64, 16, 80),
        compiler_params=PARAMS,
    )(*arrays)


def local_terms_kernel(root_ref, team_ref, stats_ref, out_ref, sums_ref):
    quad = pl.program_id(1)
    for c in range(QUAD):
        k, v = team_ref[c, 0], team_ref[c, 1]
        key_sum = value_sum = None
        for a in (c, c ^ 1, c ^ 2):
            q, d = team_ref[a, 2], team_ref[a, 3]
            top, scale, delta = (stats_ref[0, i : i + 1, head(a)] for i in range(3))
            prob = jnp.exp(dot_last(k, q) * INV_ROOT - top) * scale
            grad = dot_last(v, d)
            key_term = dot((prob * (grad - delta)).astype(jnp.bfloat16), q) * INV_ROOT
            value_term = dot(prob.astype(jnp.bfloat16), d)
            if a == c:
                key_sum, value_sum = key_term, value_term
            else:
                key_sum += key_term.astype(jnp.bfloat16).astype(jnp.float32)
                value_sum += value_term.astype(jnp.bfloat16).astype(jnp.float32)
        out_ref[c, 0] = key_sum.astype(jnp.bfloat16)
        out_ref[c, 1] = value_sum.astype(jnp.bfloat16)

        @pl.when(root_ref[0] == quad * QUAD + c)
        def _():
            sums_ref[0] = key_sum
            sums_ref[1] = value_sum


def local_terms(root_index, team, stats):
    return pl.pallas_call(
        local_terms_kernel,
        grid=(TEAM_HEADS, TEAM_SIZE // QUAD),
        in_specs=[
            SCALARS,
            pl.BlockSpec((QUAD, KINDS) + SQUARE, lambda j, i: (i, j, 0, 0)),
            pl.BlockSpec((1, STAT_ROWS, QUAD * BLOCK), lambda j, i: (j, 0, i)),
        ],
        out_specs=[
            pl.BlockSpec((QUAD, 2) + SQUARE, lambda j, i: (i, j, 0, 0)),
            pl.BlockSpec((2,) + SQUARE, lambda j, i: (j, 0, 0)),
        ],
        out_shape=[shaped((TEAM_SIZE, PARTS) + SQUARE, LOW), shaped((PARTS,) + SQUARE, FULL)],
        cost_estimate=cost(192, 48, 100),
        compiler_params=PARAMS,
    )(root_index, team, stats)


def root_kernel(index_ref, here_ref, grads_ref, sums_ref, *refs):
    out_ref = refs[-1]
    for part, ref in enumerate(refs[:-1]):
        whole = (sums_ref[part] + ref[...].astype(FULL)).astype(LOW)
        out_ref[0, part] = jnp.where(here_ref[0] == 1, whole, grads_ref[0, part])


def add_root(index, here, grads, sums, *totals):
    block = pl.BlockSpec((1, PARTS) + SQUARE, lambda i, index_ref, here_ref: (index_ref[0], 0, 0, 0))
    whole = pl.BlockSpec((PARTS,) + SQUARE, lambda i, index_ref, here_ref: (0, 0, 0))
    square = pl.BlockSpec(SQUARE, lambda i, index_ref, here_ref: (0, 0))
    return pl.pallas_call(
        root_kernel,
        grid_spec=pltpu.PrefetchScalarGridSpec(
            num_scalar_prefetch=2,
            grid=(1,),
            in_specs=[block, whole] + [square] * len(totals),
            out_specs=block,
        ),
        out_shape=shaped(grads.shape, LOW),
        input_output_aliases={2: 0},
        cost_estimate=cost(0, 0, 28),
        compiler_params=PARAMS,
    )(index, here, grads, sums, *totals)


def body(queries, keys, values, dout, global_block):
    me = lax.axis_index("ctx")
    root = global_block[0]
    index = picked(root, TEAM)
    near, far = picked(me, NEAR), picked(me, FAR)
    team_mask = sum(1 << bit for bit in TEAM)
    here = ((root | team_mask) == (me | team_mask)).astype(jnp.int32).reshape(1)
    groups_near, groups_far = 1 << len(NEAR), 1 << len(FAR)

    def others(count, k):
        return [i for i in range(count) if i != k]

    def scatter_near(k, *parts):
        got = list(parts)
        for i in others(groups_near, k):
            got[i] = sent(parts[i], NEAR, k, i)
        return spread(1, near, *got)[0]

    def send_far(k, part):
        got = [part] * groups_far
        for i in others(groups_far, k):
            got[i] = sent(part, FAR, k, i)
        return spread(groups_near, far, *got)

    def sum_far(k, part, team, stats):
        got = [part] + [sent(part, FAR, i, k) for i in others(groups_far, k)]
        return (added(got),) + tuple(local_terms(index, team, stats))

    def gather_near(k, part):
        got = [part] * groups_near
        for i in others(groups_near, k):
            got[i] = sent(part, NEAR, i, k)
        return tuple(got)

    team = split_heads(keys, values, queries, dout)
    team = exchange(team.reshape((TEAM_SIZE, TEAM_HEADS * KINDS) + SQUARE), TEAM)

    held = lax.dynamic_index_in_dim(team, index[0], 0, keepdims=False)
    part = by_root(root, NEAR, scatter_near, *(held[i] for i in (0, 1, KINDS, KINDS + 1)))
    glob = exchange(by_root(root, FAR, send_far, part), NEAR)
    sums, stats = global_terms(team, glob, local_stats(team))

    part = added(exchange(sums, NEAR))
    part, grads, local_sums = by_root(root, FAR, sum_far, part, team, stats)
    totals = by_root(root, NEAR, gather_near, part)

    grads = exchange(add_root(index, here, grads, local_sums, *totals), TEAM)
    return tuple(merge_heads(grads.reshape((HEADS, 2) + SQUARE)))


def solution(mesh):
    rows = P(("dp", "ctx"), None)
    return jax.shard_map(
        body,
        mesh=mesh,
        in_specs=(rows, rows, rows, rows, P("dp")),
        out_specs=(rows, rows),
        check_vma=False,
    )
```
